512 devices in a mesh: kvp: 64 (over z, y), head: 8 (over x, core).
Axes of the slice: x: 4, y: 8, z: 8, core: 2. Of those that a mesh axis runs over, the one named last changes fastest.
Arguments:
- stream_in: bfloat16 [8, 16384], P(None, 'kvp'), may hold values from -64 to 64
- queries: bfloat16 [8, 8, 16, 128], P(None, 'head'), may hold values from -16 to 16
- key_cache: bfloat16 [8, 8, 8192, 128], P(None, 'head', 'kvp'), may hold values from -40 to 40
- value_cache: bfloat16 [8, 8, 8192, 128], P(None, 'head', 'kvp'), may hold values from -384 to 384
- lengths: int32 [8], replicated, may hold values from 1024 to 8192, as said below
- out_weight: bfloat16 [16384, 16384], P('head', 'kvp'), may hold values from -0.046875 to 0.046875
- norm_gain: bfloat16 [16384], P('kvp'), may hold values from 0.099609375 to 1.8984375
- gate_weight: bfloat16 [16384, 26624], P('kvp', 'head'), may hold values from -0.046875 to 0.046875
- up_weight: bfloat16 [16384, 26624], P('kvp', 'head'), may hold values from -0.046875 to 0.046875
Outputs:
- stream_out: bfloat16 [8, 16384], P(None, ('kvp', 'head'))
- hidden: bfloat16 [8, 26624], P(None, 'head')
The draws below stay inside these ranges and needn't reach their ends.
Inputs may be any that keep to these rules, and one draw needn't show every extreme that they name: `lengths`: some session has exactly 8192 filled positions and some exactly 1024.
All inputs are finite; a program needn't handle non-finite values.
Results may differ from the reference program's by a relative error of at most 0.02.
Values may be sent and summed in bfloat16 or wider, within the bound.
A program may use at most 64 MiB of HBM per device.

```python
import math
import jax
import jax.numpy as jnp
from jax import lax

D = 16384
HD = 128
GROUP = 16
FF = 26624
SESS = 8
KVH = 8
HEADS = 128
POS = 8192


def draw_queries(key, part):
    key = jax.random.fold_in(key, 1)
    shape = (SESS, KVH, GROUP, HD)
    drawn = jax.random.normal(key, shape, jnp.float32)
    return jnp.clip(drawn, -16.0, 16.0).astype(jnp.bfloat16)


def draw_key_cache(key, part):
    key = jax.random.fold_in(key, 2)
    shape = (SESS, KVH, POS, HD)
    drawn = jax.random.normal(key, shape, jnp.float32)
    return jnp.clip(drawn, -40.0, 40.0).astype(jnp.bfloat16)


def draw_value_cache(key, part):
    key = jax.random.fold_in(key, 3)
    shape = (SESS, KVH, POS, HD)
    drawn = 64.0 * jax.random.normal(key, shape, jnp.float32)
    return jnp.clip(drawn, -384.0, 384.0).astype(jnp.bfloat16)


def draw_stream_in(key, part):
    key = jax.random.fold_in(key, 4)
    columns = jnp.arange(D, dtype=jnp.float32) / D
    col_scale = jnp.exp(jax.random.uniform(jax.random.fold_in(key, 21), (D,), jnp.float32, -0.5, 0.5) * math.log(10.0))
    col_scale = col_scale * 3.0 ** (columns - 0.5)
    row_scale = jnp.exp(jax.random.uniform(jax.random.fold_in(key, 22), (SESS, 1), jnp.float32, -0.5, 0.5) * math.log(10.0))
    base_draw = jax.random.normal(jax.random.fold_in(key, 23), (SESS, D), jnp.float32)
    return jnp.clip(base_draw * col_scale[None, :] * row_scale, -64.0, 64.0).astype(jnp.bfloat16)


def draw_lengths(key, part):
    key = jax.random.fold_in(key, 5)
    ranking = jax.random.permutation(jax.random.fold_in(key, 31), SESS)
    base_draw = jax.random.randint(jax.random.fold_in(key, 32), (SESS,), POS // 8, POS + 1)
    session_ids = lax.iota(jnp.int32, SESS)
    longest = ranking[0]
    shortest = ranking[1]
    picked = jnp.where(session_ids == longest, POS, jnp.where(session_ids == shortest, POS // 8, base_draw))
    return picked.astype(jnp.int32)


def block_scale(key, dims, split, least, top_value):
    def one(axis_at, blocks):
        draws = jax.random.uniform(jax.random.fold_in(jax.random.fold_in(key, 6), axis_at), (blocks,), jnp.float32, least / len(split), top_value / len(split))
        return jnp.repeat(jnp.exp(draws), dims[axis_at] // blocks).reshape((-1,) + (1,) * (len(dims) - axis_at - 1))

    gain = one(*split[0])
    for cut in split[1:]:
        gain = gain * one(*cut)
    return gain


def gaussian(key, dims, deviation, most, cuts=(), held_as=jnp.bfloat16):
    factor_of = block_scale(key, dims, cuts, -0.22, 0.18) if cuts else 1.0
    entries = jax.random.normal(key, dims, jnp.float32) * deviation * factor_of
    return jnp.minimum(jnp.maximum(entries, -most), most).astype(held_as)


def setup_inputs(seed: int = 0) -> dict:
    splits = jax.random.split(jax.random.key(seed), 10)
    stream_in = draw_stream_in(jax.random.fold_in(splits[9], 71), 0)
    queries = draw_queries(jax.random.fold_in(splits[9], 71), 0)
    key_cache = draw_key_cache(jax.random.fold_in(splits[9], 71), 0)
    value_cache = draw_value_cache(jax.random.fold_in(splits[9], 71), 0)
    lengths = draw_lengths(jax.random.fold_in(splits[9], 71), 0)
    out_weight = gaussian(splits[5], (HEADS * HD, D), (HEADS * HD) ** -0.5, 0.046875, ((0, 8), (1, 64)))
    norm_gain = jnp.clip(1.0 + 0.18 * jax.random.normal(splits[6], (D,), jnp.float32), 0.099609375, 1.8984375).astype(jnp.bfloat16)
    gate_weight = gaussian(splits[7], (D, FF), D ** -0.5, 0.046875, ((0, 64), (1, 8)))
    up_weight = gaussian(splits[8], (D, FF), D ** -0.5, 0.046875, ((0, 64), (1, 8)))
    return {"stream_in": stream_in, "queries": queries, "key_cache": key_cache, "value_cache": value_cache, "lengths": lengths, "out_weight": out_weight, "norm_gain": norm_gain, "gate_weight": gate_weight, "up_weight": up_weight}


neg_fill = -1e+30
epsilon = 1e-05

def attend(session_items):
    query_rows, key_rows, value_rows, length = session_items
    scores = jnp.einsum('gjd,gpd->gjp', query_rows.astype(jnp.float32), key_rows.astype(jnp.float32)) * HD ** (-0.5)
    included = jnp.arange(POS, dtype=jnp.int32)[None, None, :] < length
    scores = jnp.where(included, scores, neg_fill)
    top_score = lax.optimization_barrier(jnp.max(scores, axis=2, keepdims=True))
    weights = jnp.where(included, jnp.exp(scores - top_score), 0.0)
    weight_sum = lax.optimization_barrier(jnp.sum(weights, axis=2, keepdims=True))
    weighted = jnp.einsum('gjp,gpd->gjd', weights, value_rows.astype(jnp.float32))
    return weighted / weight_sum

def reference(stream_in, queries, key_cache, value_cache, lengths, out_weight, norm_gain, gate_weight, up_weight):
    attended = lax.map(attend, (queries, key_cache, value_cache, lengths))
    attended = attended.astype(jnp.bfloat16).reshape(SESS, HEADS * HD)
    projected = jnp.dot(attended, out_weight, preferred_element_type=jnp.float32)
    stream_out = (stream_in.astype(jnp.float32) + projected).astype(jnp.bfloat16)
    widened = stream_out.astype(jnp.float32)
    square_sum = lax.optimization_barrier(jnp.sum(widened * widened, axis=1))
    inverse = lax.rsqrt(square_sum / D + epsilon)
    normed = (widened * inverse[:, None] * norm_gain.astype(jnp.float32)).astype(jnp.bfloat16)
    gate = jnp.dot(normed, gate_weight, preferred_element_type=jnp.float32)
    upward = jnp.dot(normed, up_weight, preferred_element_type=jnp.float32)
    hidden = (jax.nn.silu(gate) * upward).astype(jnp.bfloat16)
    return (stream_out, hidden)
```

```python
import jax
import jax.numpy as jnp
from jax import lax
from jax.experimental import pallas as pl
from jax.experimental.pallas import tpu as pltpu
from jax.sharding import PartitionSpec as P

D = 16384
neg_fill = -1e30
epsilon = 1e-05
MESH = pl.DeviceIdType.MESH
FAR_FIRST = (4, 3, 5, 2, 6, 1, 7)
F32 = jnp.float32
BF16 = jnp.bfloat16


def merge(parts, axis):
    total = parts[:, 0:8, :]
    stats = parts[:, 8:16, :]
    turned = jnp.concatenate([stats[:, :, 64:], stats[:, :, :64]], axis=2)
    low = lax.broadcasted_iota(jnp.int32, stats.shape, 2) < 64
    shift = jnp.where(low, stats, turned)
    weight = jnp.where(low, turned, stats)
    top = jnp.max(shift, axis=0)
    scale = jnp.exp(shift - top[None])
    return jnp.sum(scale * total, axis=0), top, jnp.sum(scale * weight, axis=0)


def pack_stats(total, top, weight):
    low = lax.broadcasted_iota(jnp.int32, top.shape, 1) < 64
    return jnp.concatenate([total, jnp.where(low, top, weight)], axis=0).astype(BF16)


def kernel(
    stream_hbm, q_hbm, k_hbm, v_hbm, len_hbm, ow_hbm, gain_hbm, gw_hbm, uw_hbm,
    so_ref, hid_ref,
    stream_ref, q_ref, k_ref, v_ref, len_ref, ow_ref, gain_ref, gw_ref, uw_ref, in_sem,
    a1_send, a1_recv, a2_send, a2_recv, a3_send, a3_recv,
    h_send, h_recv, d1_send, d1_recv, d2_send, d2_recv, d3_send, d3_recv,
    send_sem, recv_sem,
):
    kvp, head = lax.axis_index("kvp"), lax.axis_index("head")
    z, y = kvp // 8, lax.rem(kvp, 8)

    def at_z(p):
        return (p * 8 + y, head)

    def at_y(p):
        return (z * 8 + p, head)

    def at_head(p):
        return (kvp, p)

    axes = ((z, at_z), (y, at_y))

    barrier = pltpu.get_barrier_semaphore()
    for me, at in axes + ((head, at_head),):
        for d in FAR_FIRST:
            pl.semaphore_signal(barrier, inc=1, device_id=at(lax.rem(me + d, 8)), device_id_type=MESH)

    loads = {}
    for n, (name, src, dst) in enumerate((
        ("len", len_hbm, len_ref), ("q", q_hbm, q_ref), ("k", k_hbm, k_ref), ("v", v_hbm, v_ref),
        ("stream", stream_hbm, stream_ref), ("gain", gain_hbm, gain_ref),
        ("ow", ow_hbm, ow_ref), ("gw", gw_hbm, gw_ref), ("uw", uw_hbm, uw_ref),
    )):
        loads[name] = pltpu.make_async_copy(src, dst, in_sem.at[n])
        loads[name].start()

    def send(phase, axis, src_of, recv):
        me, at = axis
        for d in FAR_FIRST:
            p = lax.rem(me + d, 8)
            pltpu.make_async_remote_copy(
                src_of(p), recv.at[me], send_sem.at[phase], recv_sem.at[phase], device_id=at(p), device_id_type=MESH
            ).start()

    def arrived(phase, recv):
        seven = recv.at[pl.ds(0, 7)]
        pltpu.make_async_copy(seven, seven, recv_sem.at[phase]).wait()

    for name in ("len", "q", "k", "v"):
        loads[name].wait()
    lane = lax.broadcasted_iota(jnp.int32, (16, 128), 1)
    position = kvp * 128 + lane
    low = lane < 64
    for s in range(8):
        score = lax.dot_general(
            q_ref[s], k_ref[s], (((1,), (1,)), ((), ())), preferred_element_type=F32
        ) * (128**-0.5)
        inside = position < len_ref[s]
        score = jnp.where(inside, score, neg_fill)
        top = jnp.max(score, axis=1, keepdims=True).astype(BF16).astype(F32)
        weight = jnp.where(inside, jnp.exp(score - top), 0.0).astype(BF16)
        weight_sum = jnp.sum(weight.astype(F32), axis=1, keepdims=True)
        total = jnp.dot(weight, v_ref[s], preferred_element_type=F32)
        stats = jnp.where(low, top, weight_sum)
        for j in range(2):
            rows = slice(8 * j, 8 * j + 8)
            a1_send[s // 4, (s % 4) * 2 + j] = jnp.concatenate([total[rows], stats[rows]], axis=0).astype(BF16)

    pl.semaphore_wait(barrier, 21)
    for f in range(2):
        send(f, axes[f], lambda p: a1_send.at[f, p], a1_recv.at[f])
        me = axes[f][0]
        a1_recv[f, me] = a1_send[f, me]
    for f in range(2):
        arrived(f, a1_recv.at[f])
        a2_send[f] = pack_stats(*merge(a1_recv[f].astype(F32), f))
        send(2 + f, axes[1 - f], lambda p: a2_send.at[f], a2_recv.at[f])
        a2_recv[f, axes[1 - f][0]] = a2_send[f]
    for f in range(2):
        arrived(2 + f, a2_recv.at[f])
        total, _, weight = merge(a2_recv[f].astype(F32), f)
        a3_send[f] = (total / weight).astype(BF16).astype(F32)
        send(4 + f, axes[f], lambda p: a3_send.at[f], a3_recv.at[pl.ds(8 * f, 8)])
        a3_recv[8 * f + axes[f][0]] = a3_send[f]
    for f in range(2):
        arrived(4 + f, a3_recv.at[pl.ds(8 * f, 8)])

    loads["ow"].wait()
    loads["stream"].wait()
    loads["gain"].wait()
    rows = a3_recv[...].reshape(8, 16, 128)
    attended = jnp.concatenate([rows[:, j, :] for j in range(16)], axis=1).astype(BF16)
    h_send[...] = jnp.dot(attended, ow_ref[...], preferred_element_type=F32)
    send(6, (head, at_head), lambda p: h_send, h_recv)
    h_recv[head] = h_send[...]
    arrived(6, h_recv)
    projected = jnp.sum(h_recv[...], axis=0)
    stream_out = (stream_ref[...].astype(F32) + projected).astype(BF16)
    so_ref[...] = stream_out
    widened = stream_out.astype(F32)
    square = jnp.broadcast_to(jnp.sum(widened * widened, axis=1, keepdims=True), (8, 128))
    scaled = (widened * gain_ref[...].astype(F32)).astype(BF16)

    loads["gw"].wait()
    loads["uw"].wait()
    high = square.astype(BF16)
    squares = jnp.concatenate([square, square - high.astype(F32)], axis=0).astype(BF16)

    def eighth(f, k):
        columns = pl.ds(pl.multiple_of((13 * f + (13 * k) // 8) * 128, 128), 256)
        gate = jnp.dot(scaled, gw_ref[:, columns], preferred_element_type=F32)
        up = jnp.dot(scaled, uw_ref[:, columns], preferred_element_type=F32)
        return jnp.concatenate([jnp.concatenate([gate, up], axis=0).astype(BF16), squares], axis=1)

    for d in FAR_FIRST:
        for f in range(2):
            me, at = axes[f]
            p = lax.rem(me + d, 8)
            d1_send[f, p] = eighth(f, p)
            pltpu.make_async_remote_copy(
                d1_send.at[f, p], d1_recv.at[f, me], send_sem.at[7 + f], recv_sem.at[7 + f],
                device_id=at(p), device_id_type=MESH,
            ).start()
    for f in range(2):
        me = axes[f][0]
        d1_recv[f, me] = eighth(f, me)
    for f in range(2):
        arrived(7 + f, d1_recv.at[f])
        part = jnp.sum(d1_recv[f].astype(F32), axis=0)
        square = part[0:8, 256:] + part[8:16, 256:]
        rest = square - square.astype(BF16).astype(F32)
        part = jnp.concatenate([part[:, :256], jnp.concatenate([square, rest], axis=0)], axis=1)
        d2_send[f] = part.astype(BF16)
        send(9 + f, axes[1 - f], lambda p: d2_send.at[f], d2_recv.at[f])
        d2_recv[f, axes[1 - f][0]] = d2_send[f]
    for f in range(2):
        arrived(9 + f, d2_recv.at[f])
        part = jnp.sum(d2_recv[f].astype(F32), axis=0)
        square = part[0:8, 256:] + part[8:16, 256:]
        inverse = lax.rsqrt(square / D + epsilon)
        inverse = jnp.concatenate([inverse, inverse], axis=1)
        gate, up = part[0:8, :256] * inverse, part[8:16, :256] * inverse
        hidden = gate / (1.0 + jnp.exp(-gate)) * up
        d3_send[f] = jnp.concatenate([hidden[:, :128], hidden[:, 128:]], axis=0).astype(BF16)
        send(11 + f, axes[f], lambda p: d3_send.at[f], d3_recv.at[f])
        d3_recv[f, axes[f][0]] = d3_send[f]
    for f in range(2):
        arrived(11 + f, d3_recv.at[f])
        for t in range(13):
            k = max(k for k in range(8) if 13 * k // 8 <= t)
            half = t - 13 * k // 8
            hid_ref[:, (13 * f + t) * 128 : (13 * f + t + 1) * 128] = d3_recv[f, k, 8 * half : 8 * half + 8, :]

    for f in range(2):
        for phase, buffer in (
            (f, a1_send.at[f, pl.ds(0, 7)]),
            (2 + f, a1_send.at[f, pl.ds(0, 7)]),
            (4 + f, a3_recv.at[pl.ds(0, 7)]),
            (7 + f, d1_send.at[f, pl.ds(0, 7)]),
            (9 + f, d1_send.at[f, pl.ds(0, 7)]),
            (11 + f, d3_recv.at[f, pl.ds(0, 7)]),
        ):
            pltpu.make_async_copy(buffer, buffer, send_sem.at[phase]).wait()
    seven = h_recv.at[pl.ds(0, 7)]
    pltpu.make_async_copy(seven, seven, send_sem.at[6]).wait()


def body(stream_in, queries, key_cache, value_cache, lengths, out_weight, norm_gain, gate_weight, up_weight):
    vmem, dma = pltpu.VMEM, pltpu.SemaphoreType.DMA
    residual, hidden = pl.pallas_call(
        kernel,
        out_shape=(jax.ShapeDtypeStruct((8, 256), BF16), jax.ShapeDtypeStruct((8, 3328), BF16)),
        in_specs=[pl.BlockSpec(memory_space=pl.ANY)] * 9,
        out_specs=(pl.BlockSpec(memory_space=vmem), pl.BlockSpec(memory_space=vmem)),
        scratch_shapes=[
            vmem((8, 256), BF16),
            vmem((8, 16, 128), BF16),
            vmem((8, 128, 128), BF16),
            vmem((8, 128, 128), BF16),
            pltpu.SMEM((8,), jnp.int32),
            vmem((2048, 256), BF16),
            vmem((1, 256), BF16),
            vmem((256, 3328), BF16),
            vmem((256, 3328), BF16),
            dma((9,)),
            vmem((2, 8, 16, 128), BF16),
            vmem((2, 8, 16, 128), BF16),
            vmem((2, 16, 128), BF16),
            vmem((2, 8, 16, 128), BF16),
            vmem((2, 8, 128), F32),
            vmem((16, 8, 128), F32),
            vmem((8, 256), F32),
            vmem((8, 8, 256), F32),
            vmem((2, 8, 16, 384), BF16),
            vmem((2, 8, 16, 384), BF16),
            vmem((2, 16, 384), BF16),
            vmem((2, 8, 16, 384), BF16),
            vmem((2, 16, 128), BF16),
            vmem((2, 8, 16, 128), BF16),
            dma((13,)),
            dma((13,)),
        ],
        compiler_params=pltpu.CompilerParams(
            collective_id=0, has_side_effects=True, vmem_limit_bytes=60 * 1024 * 1024
        ),
        name="decode_step",
    )(
        stream_in, queries[:, 0], key_cache[:, 0], value_cache[:, 0], lengths, out_weight,
        norm_gain.reshape(1, 256), gate_weight, up_weight,
    )
    stream_out = lax.dynamic_slice_in_dim(residual, lax.axis_index("head") * 32, 32, 1)
    return stream_out, hidden


def solution(mesh):
    return jax.shard_map(
        body,
        mesh=mesh,
        in_specs=(
            P(None, "kvp"),
            P(None, "head", None, None),
            P(None, "head", "kvp", None),
            P(None, "head", "kvp", None),
            P(),
            P("head", "kvp"),
            P("kvp"),
            P("kvp", "head"),
            P("kvp", "head"),
        ),
        out_specs=(P(None, ("kvp", "head")), P(None, "head")),
        check_vma=False,
    )
```

```python
import jax
import jax.numpy as jnp
from jax import lax
from jax.experimental import pallas as pl
from jax.experimental.pallas import tpu as pltpu
from jax.sharding import PartitionSpec as P

D = 16384
neg_fill = -1e30
epsilon = 1e-05
MESH = pl.DeviceIdType.MESH
F32 = jnp.float32
BF16 = jnp.bfloat16


def merge(parts):
    stats = parts[:, 64:80, :].astype(F32)
    shift = jnp.max(stats, axis=0)
    scale = jnp.exp(stats - shift[None])
    weight = jnp.sum(scale * pltpu.roll(stats.reshape(128, 128), 112, 1).reshape(8, 16, 128), axis=0)
    totals = []
    for s in range(4):
        total = None
        for k in range(8):
            term = scale[k, :, 32 * s : 32 * s + 1] * parts[k, 16 * s : 16 * s + 16, :].astype(F32)
            total = term if total is None else total + term
        totals.append(total)
    return totals, shift, weight


def kernel(
    stream_hbm, q_hbm, k_hbm, v_hbm, len_hbm, ow_hbm, gain_hbm, gw_hbm, uw_hbm,
    so_ref, hid_ref,
    stream_ref, q_ref, k_ref, v_ref, len_ref, ow_ref, gain_ref, gw_ref, uw_ref, in_sem,
    a1_send, a1_recv, a2_send, a2_recv, rows,
    h_send, h_recv, d1_send, d1_recv, d2_send, d2_recv, d3_send, d3_recv,
    send_sem, recv_sem,
):
    kvp, head = lax.axis_index("kvp"), lax.axis_index("head")
    z, y = kvp // 8, lax.rem(kvp, 8)

    def at_z(p):
        return (p * 8 + y, head)

    def at_y(p):
        return (z * 8 + p, head)

    def at_head(p):
        return (kvp, p)

    def place(f):
        return jnp.where(f == 0, z, y)

    def at(f, p):
        return (jnp.where(f == 0, p * 8 + y, z * 8 + p), head)

    def far_first(me, n):
        half = (n + 1) // 2
        return lax.rem(me + jnp.where(lax.rem(n, 2) == 0, 4 + half, 4 - half), 8)

    barrier = pltpu.get_barrier_semaphore()

    @pl.loop(0, 7)
    def _(n):
        for target in (at_z(far_first(z, n)), at_y(far_first(y, n)), at_head(far_first(head, n))):
            pl.semaphore_signal(barrier, inc=1, device_id=target, device_id_type=MESH)

    loads = {}
    for n, (name, src, dst) in enumerate((
        ("len", len_hbm, len_ref), ("q", q_hbm, q_ref), ("k", k_hbm, k_ref), ("v", v_hbm, v_ref),
        ("stream", stream_hbm, stream_ref), ("gain", gain_hbm, gain_ref),
        ("ow", ow_hbm, ow_ref), ("gw", gw_hbm, gw_ref), ("uw", uw_hbm, uw_ref),
    )):
        loads[name] = pltpu.make_async_copy(src, dst, in_sem.at[n])
        loads[name].start()

    def send(phase, f, src_of, recv):
        me = place(f)

        @pl.loop(0, 7)
        def _(n):
            p = far_first(me, n)
            pltpu.make_async_remote_copy(
                src_of(p), recv.at[me], send_sem.at[phase], recv_sem.at[phase], device_id=at(f, p), device_id_type=MESH
            ).start()

    def arrived(phase, recv):
        seven = recv.at[pl.ds(0, 7)]
        pltpu.make_async_copy(seven, seven, recv_sem.at[phase]).wait()

    for name in ("len", "q", "k", "v"):
        loads[name].wait()
    lane = lax.broadcasted_iota(jnp.int32, (16, 128), 1)
    position = kvp * 128 + lane
    for f in range(2):
        stats = jnp.zeros((16, 128), F32)
        for s in range(4):
            score = lax.dot_general(
                q_ref[4 * f + s], k_ref[4 * f + s], (((1,), (1,)), ((), ())), preferred_element_type=F32
            ) * (128**-0.5)
            inside = position < len_ref[4 * f + s]
            score = jnp.where(inside, score, neg_fill)
            top = jnp.max(score, axis=1, keepdims=True).astype(BF16).astype(F32)
            weight = jnp.where(inside, jnp.exp(score - top), 0.0).astype(BF16)
            weight_sum = jnp.sum(weight.astype(F32), axis=1, keepdims=True)
            total = jnp.dot(weight, v_ref[4 * f + s], preferred_element_type=F32)
            a1_send[f, 16 * s : 16 * s + 16] = total.astype(BF16)
            stats = jnp.where(lane // 16 == 2 * s, top, jnp.where(lane // 16 == 2 * s + 1, weight_sum, stats))
        a1_send[f, 64:80] = stats.astype(BF16)

    pl.semaphore_wait(barrier, 21)

    @pl.loop(0, 2)
    def _(f):
        send(f, f, lambda p: a1_send.at[f], a1_recv.at[f])
        a1_recv[f, place(f)] = a1_send[f]


    @pl.loop(0, 2)
    def _(f):
        arrived(f, a1_recv.at[f])
        totals, shift, weight = merge(a1_recv[f])
        for s in range(4):
            a2_send[f, 16 * s : 16 * s + 16] = totals[s].astype(BF16)
        a2_send[f, 64:80] = jnp.where(lax.rem(lane // 16, 2) == 0, shift, pltpu.roll(weight, 16, 1)).astype(BF16)
        send(2 + f, 1 - f, lambda p: a2_send.at[f], a2_recv.at[f])
        a2_recv[f, place(1 - f)] = a2_send[f]

    @pl.loop(0, 2)
    def _(f):
        arrived(2 + f, a2_recv.at[f])
        totals, _, weight = merge(a2_recv[f])
        inverse = 1.0 / weight
        for s in range(4):
            rows[pl.ds(64 * f + 16 * s, 16)] = totals[s] * inverse[:, 32 * s : 32 * s + 1]

    loads["ow"].wait()
    loads["stream"].wait()
    loads["gain"].wait()
    attended = jnp.concatenate([rows[pl.ds(j, 8, stride=16), :] for j in range(16)], axis=1).astype(BF16)
    h_send[...] = jnp.dot(attended, ow_ref[...], preferred_element_type=F32)

    @pl.loop(0, 7)
    def _(n):
        p = far_first(head, n)
        pltpu.make_async_remote_copy(
            h_send, h_recv.at[head], send_sem.at[6], recv_sem.at[6], device_id=at_head(p), device_id_type=MESH
        ).start()

    h_recv[head] = h_send[...]
    arrived(6, h_recv)
    projected = jnp.sum(h_recv[...], axis=0)
    stream_out = (stream_ref[...].astype(F32) + projected).astype(BF16)
    so_ref[...] = stream_out
    widened = stream_out.astype(F32)
    square = jnp.broadcast_to(jnp.sum(widened * widened, axis=1, keepdims=True), (8, 128))
    scaled = (widened * gain_ref[...].astype(F32).reshape(1, 256)).astype(BF16)

    loads["gw"].wait()
    loads["uw"].wait()
    high = square.astype(BF16)
    squares = jnp.concatenate([square, square - high.astype(F32)], axis=0).astype(BF16)

    def eighth(f, k):
        columns = pl.ds(pl.multiple_of((13 * f + (13 * k) // 8) * 128, 128), 256)
        gate = jnp.dot(scaled, gw_ref[:, columns], preferred_element_type=F32)
        up = jnp.dot(scaled, uw_ref[:, columns], preferred_element_type=F32)
        return jnp.concatenate([jnp.concatenate([gate, up], axis=0).astype(BF16), squares], axis=1)

    @pl.loop(0, 8)
    def _(n):
        for f in range(2):
            me = place(f)
            p = far_first(me, n)
            d1_send[f, p] = eighth(f, p)

            @pl.when(n < 7)
            def _():
                pltpu.make_async_remote_copy(
                    d1_send.at[f, p], d1_recv.at[f, me], send_sem.at[7 + f], recv_sem.at[7 + f],
                    device_id=at(f, p), device_id_type=MESH,
                ).start()

    @pl.loop(0, 2)
    def _(f):
        d1_recv[f, place(f)] = d1_send[f, place(f)]
        arrived(7 + f, d1_recv.at[f])
        part = jnp.sum(d1_recv[f].astype(F32), axis=0)
        square = part[0:8, 256:] + part[8:16, 256:]
        rest = square - square.astype(BF16).astype(F32)
        part = jnp.concatenate([part[:, :256], jnp.concatenate([square, rest], axis=0)], axis=1)
        d2_send[f] = part.astype(BF16)
        send(9 + f, 1 - f, lambda p: d2_send.at[f], d2_recv.at[f])
        d2_recv[f, place(1 - f)] = d2_send[f]

    @pl.loop(0, 2)
    def _(f):
        arrived(9 + f, d2_recv.at[f])
        part = jnp.sum(d2_recv[f].astype(F32), axis=0)
        square = part[0:8, 256:] + part[8:16, 256:]
        inverse = lax.rsqrt(square / D + epsilon)
        inverse = jnp.concatenate([inverse, inverse], axis=1)
        gate, up = part[0:8, :256] * inverse, part[8:16, :256] * inverse
        hidden = gate / (1.0 + jnp.exp(-gate)) * up
        d3_send[f] = jnp.concatenate([hidden[:, :128], hidden[:, 128:]], axis=0).astype(BF16)
        send(11 + f, f, lambda p: d3_send.at[f], d3_recv.at[f])
        d3_recv[f, place(f)] = d3_send[f]

    for f in range(2):
        arrived(11 + f, d3_recv.at[f])
        for t in range(13):
            k = max(k for k in range(8) if 13 * k // 8 <= t)
            half = t - 13 * k // 8
            hid_ref[:, (13 * f + t) * 128 : (13 * f + t + 1) * 128] = d3_recv[f, k, 8 * half : 8 * half + 8, :]

    for f in range(2):
        for phase, buffer in (
            (f, a1_recv.at[f, pl.ds(0, 7)]),
            (2 + f, a2_recv.at[f, pl.ds(0, 7)]),
            (7 + f, d1_send.at[f, pl.ds(0, 7)]),
            (9 + f, d1_send.at[f, pl.ds(0, 7)]),
            (11 + f, d3_recv.at[f, pl.ds(0, 7)]),
        ):
            pltpu.make_async_copy(buffer, buffer, send_sem.at[phase]).wait()
    seven = h_recv.at[pl.ds(0, 7)]
    pltpu.make_async_copy(seven, seven, send_sem.at[6]).wait()


def body(stream_in, queries, key_cache, value_cache, lengths, out_weight, norm_gain, gate_weight, up_weight):
    vmem, dma = pltpu.VMEM, pltpu.SemaphoreType.DMA
    residual, hidden = pl.pallas_call(
        kernel,
        out_shape=(vmem((8, 256), BF16), vmem((8, 3328), BF16)),
        in_specs=[pl.BlockSpec(memory_space=pl.ANY)] * 9,
        out_specs=(pl.BlockSpec(memory_space=vmem), pl.BlockSpec(memory_space=vmem)),
        scratch_shapes=[
            vmem((8, 256), BF16),
            vmem((8, 16, 128), BF16),
            vmem((8, 128, 128), BF16),
            vmem((8, 128, 128), BF16),
            pltpu.SMEM((8,), jnp.int32),
            vmem((2048, 256), BF16),
            vmem((256,), BF16),
            vmem((256, 3328), BF16),
            vmem((256, 3328), BF16),
            dma((9,)),
            vmem((2, 80, 128), BF16),
            vmem((2, 8, 80, 128), BF16),
            vmem((2, 80, 128), BF16),
            vmem((2, 8, 80, 128), BF16),
            vmem((128, 128), F32),
            vmem((8, 256), F32),
            vmem((8, 8, 256), F32),
            vmem((2, 8, 16, 384), BF16),
            vmem((2, 8, 16, 384), BF16),
            vmem((2, 16, 384), BF16),
            vmem((2, 8, 16, 384), BF16),
            vmem((2, 16, 128), BF16),
            vmem((2, 8, 16, 128), BF16),
            dma((13,)),
            dma((13,)),
        ],
        compiler_params=pltpu.CompilerParams(
            collective_id=0, has_side_effects=True, vmem_limit_bytes=40 * 1024 * 1024
        ),
        name="decode_step",
    )(
        *(pltpu.with_memory_space_constraint(a, pltpu.HBM) for a in (stream_in, queries[:, 0], key_cache[:, 0], value_cache[:, 0], lengths, out_weight,
        norm_gain, gate_weight, up_weight)),
    )
    stream_out = lax.dynamic_slice_in_dim(residual, lax.axis_index("head") * 32, 32, 1)
    return stream_out, hidden


def solution(mesh):
    return jax.shard_map(
        body,
        mesh=mesh,
        in_specs=(
            P(None, "kvp"),
            P(None, "head", None, None),
            P(None, "head", "kvp", None),
            P(None, "head", "kvp", None),
            P(),
            P("head", "kvp"),
            P("kvp"),
            P("kvp", "head"),
            P("kvp", "head"),
        ),
        out_specs=(P(None, ("kvp", "head")), P(None, "head")),
        check_vma=False,
    )
```

```python
import jax
import jax.numpy as jnp
from jax import lax
from jax.experimental import pallas as pl
from jax.experimental.pallas import tpu as pltpu
from jax.sharding import PartitionSpec as P

D = 16384
neg_fill = -1e30
epsilon = 1e-05
MESH = pl.DeviceIdType.MESH
F32 = jnp.float32
BF16 = jnp.bfloat16


def merge(parts):
    stats = parts[:, 64:80, :].astype(F32)
    shift = jnp.max(stats, axis=0)
    scale = jnp.exp(stats - shift[None])
    weight = jnp.sum(scale * pltpu.roll(stats.reshape(128, 128), 112, 1).reshape(8, 16, 128), axis=0)
    totals = []
    for s in range(4):
        total = None
        for k in range(8):
            term = scale[k, :, 32 * s : 32 * s + 1] * parts[k, 16 * s : 16 * s + 16, :].astype(F32)
            total = term if total is None else total + term
        totals.append(total)
    return totals, shift, weight


def kernel(
    stream_hbm, q_hbm, k_hbm, v_hbm, len_hbm, ow_hbm, gain_hbm, gw_hbm, uw_hbm,
    so_ref, hid_ref,
    stream_ref, q_ref, k_ref, v_ref, len_ref, ow_ref, gain_ref, gw_ref, uw_ref, in_sem,
    a1_send, a1_recv, a2_send, a2_recv, rows,
    h_send, h_recv, d1_send, d1_recv, d2_send, d2_recv, d3_send, d3_recv,
    send_sem, recv_sem,
):
    kvp, head = lax.axis_index("kvp"), lax.axis_index("head")
    z, y = kvp // 8, lax.rem(kvp, 8)

    def at_z(p):
        return (p * 8 + y, head)

    def at_y(p):
        return (z * 8 + p, head)

    def at_head(p):
        return (kvp, p)

    def place(f):
        return jnp.where(f == 0, z, y)

    def at(f, p):
        return (jnp.where(f == 0, p * 8 + y, z * 8 + p), head)

    def far_first(me, n):
        half = (n + 1) // 2
        return lax.rem(me + jnp.where(lax.rem(n, 2) == 0, 4 + half, 4 - half), 8)

    loads = {}
    for n, (name, src, dst) in enumerate((
        ("k", k_hbm, k_ref), ("q", q_hbm, q_ref), ("len", len_hbm, len_ref), ("v", v_hbm, v_ref),
        ("stream", stream_hbm, stream_ref), ("gain", gain_hbm, gain_ref),
        ("ow", ow_hbm, ow_ref), ("gw", gw_hbm, gw_ref), ("uw", uw_hbm, uw_ref),
    )):
        loads[name] = pltpu.make_async_copy(src, dst, in_sem.at[n])
        if n < 4:
            loads[name].start()

    barrier = pltpu.get_barrier_semaphore()

    @pl.loop(0, 7)
    def _(n):
        for target in (at_z(far_first(z, n)), at_y(far_first(y, n)), at_head(far_first(head, n))):
            pl.semaphore_signal(barrier, inc=1, device_id=target, device_id_type=MESH)

    for name in ("stream", "gain", "ow", "gw", "uw"):
        loads[name].start()

    def send(phase, f, src_of, recv):
        me = place(f)

        @pl.loop(0, 7)
        def _(n):
            p = far_first(me, n)
            pltpu.make_async_remote_copy(
                src_of(p), recv.at[me], send_sem.at[phase], recv_sem.at[phase], device_id=at(f, p), device_id_type=MESH
            ).start()

    def arrived(phase, recv):
        seven = recv.at[pl.ds(0, 7)]
        pltpu.make_async_copy(seven, seven, recv_sem.at[phase]).wait()

    for name in ("len", "q", "k", "v"):
        loads[name].wait()
    lane = lax.broadcasted_iota(jnp.int32, (16, 128), 1)
    position = kvp * 128 + lane
    for f in range(2):
        stats = jnp.zeros((16, 128), F32)
        for s in range(4):
            score = lax.dot_general(
                q_ref[4 * f + s], k_ref[4 * f + s], (((1,), (1,)), ((), ())), preferred_element_type=F32
            ) * (128**-0.5)
            inside = position < len_ref[4 * f + s]
            score = jnp.where(inside, score, neg_fill)
            top = jnp.max(score, axis=1, keepdims=True).astype(BF16).astype(F32)
            weight = jnp.where(inside, jnp.exp(score - top), 0.0).astype(BF16)
            weight_sum = jnp.sum(weight.astype(F32), axis=1, keepdims=True)
            total = jnp.dot(weight, v_ref[4 * f + s], preferred_element_type=F32)
            a1_send[f, 16 * s : 16 * s + 16] = total.astype(BF16)
            stats = jnp.where(lane // 16 == 2 * s, top, jnp.where(lane // 16 == 2 * s + 1, weight_sum, stats))
        a1_send[f, 64:80] = stats.astype(BF16)

    pl.semaphore_wait(barrier, 21)

    @pl.loop(0, 2)
    def _(f):
        send(f, f, lambda p: a1_send.at[f], a1_recv.at[f])
        a1_recv[f, place(f)] = a1_send[f]


    @pl.loop(0, 2)
    def _(f):
        arrived(f, a1_recv.at[f])
        totals, shift, weight = merge(a1_recv[f])
        for s in range(4):
            a2_send[f, 16 * s : 16 * s + 16] = totals[s].astype(BF16)
        a2_send[f, 64:80] = jnp.where(lax.rem(lane // 16, 2) == 0, shift, pltpu.roll(weight, 16, 1)).astype(BF16)
        send(2 + f, 1 - f, lambda p: a2_send.at[f], a2_recv.at[f])
        a2_recv[f, place(1 - f)] = a2_send[f]

    @pl.loop(0, 2)
    def _(f):
        arrived(2 + f, a2_recv.at[f])
        totals, _, weight = merge(a2_recv[f])
        inverse = 1.0 / weight
        for s in range(4):
            rows[pl.ds(64 * f + 16 * s, 16)] = totals[s] * inverse[:, 32 * s : 32 * s + 1]

    loads["ow"].wait()
    loads["stream"].wait()
    loads["gain"].wait()
    attended = jnp.concatenate([rows[pl.ds(j, 8, stride=16), :] for j in range(16)], axis=1).astype(BF16)
    h_send[...] = jnp.dot(attended, ow_ref[...], preferred_element_type=F32)

    @pl.loop(0, 7)
    def _(n):
        p = far_first(head, n)
        pltpu.make_async_remote_copy(
            h_send, h_recv.at[head], send_sem.at[6], recv_sem.at[6], device_id=at_head(p), device_id_type=MESH
        ).start()

    h_recv[head] = h_send[...]
    arrived(6, h_recv)
    projected = jnp.sum(h_recv[...], axis=0)
    stream_out = (stream_ref[...].astype(F32) + projected).astype(BF16)
    widened = stream_out.astype(F32)
    so_ref[...] = pltpu.roll(widened, lax.rem(8 - head, 8) * 32, 1)[:, :32].astype(BF16)
    square = jnp.broadcast_to(jnp.sum(widened * widened, axis=1, keepdims=True), (8, 128))
    scaled = (widened * gain_ref[...].astype(F32).reshape(1, 256)).astype(BF16)

    high = square.astype(BF16)
    squares = jnp.concatenate([square, square - high.astype(F32)], axis=0).astype(BF16)
    for f in range(2):
        d1_send[f, 7] = jnp.concatenate([squares, squares], axis=1)
    loads["gw"].wait()
    loads["uw"].wait()

    def split_squares(f, part):
        square = part[0:8] + part[8:16]
        terms = jnp.concatenate([square, square - square.astype(BF16).astype(F32)], axis=0)
        return jnp.where(place(f) == 7, terms, part).astype(BF16)

    @pl.loop(0, 8)
    def _(n):
        for f in range(2):
            me = place(f)
            p = far_first(me, n)

            @pl.when(p < 7)
            def _():
                columns = pl.ds(pl.multiple_of((13 * f + jnp.minimum(2 * p, 11)) * 128, 128), 256)
                gate = jnp.dot(scaled, gw_ref[:, columns], preferred_element_type=F32)
                up = jnp.dot(scaled, uw_ref[:, columns], preferred_element_type=F32)
                d1_send[f, p] = jnp.concatenate([gate, up], axis=0).astype(BF16)

            @pl.when(n < 7)
            def _():
                pltpu.make_async_remote_copy(
                    d1_send.at[f, p], d1_recv.at[f, me], send_sem.at[7 + f], recv_sem.at[7 + f],
                    device_id=at(f, p), device_id_type=MESH,
                ).start()

    @pl.loop(0, 2)
    def _(f):
        d1_recv[f, place(f)] = d1_send[f, place(f)]
        arrived(7 + f, d1_recv.at[f])
        d2_send[f] = split_squares(f, jnp.sum(d1_recv[f].astype(F32), axis=0))
        send(9 + f, 1 - f, lambda p: d2_send.at[f], d2_recv.at[f])
        d2_recv[f, place(1 - f)] = d2_send[f]

    @pl.loop(0, 2)
    def _(f):
        arrived(9 + f, d2_recv.at[f])
        d3_send[f] = split_squares(f, jnp.sum(d2_recv[f].astype(F32), axis=0))
        send(11 + f, f, lambda p: d3_send.at[f], d3_recv.at[f])
        d3_recv[f, place(f)] = d3_send[f]

    for f in range(2):
        arrived(11 + f, d3_recv.at[f])
    square = d3_recv[0, 7, :, 0:128].astype(F32)
    inverse = lax.rsqrt((square[0:8] + square[8:16]) / D + epsilon)
    for f in range(2):
        for t in range(13):
            k = min(t // 2, 6)
            at_column = (t - min(2 * k, 11)) * 128
            both = d3_recv[f, k, :, at_column : at_column + 128].astype(F32)
            gate, up = both[0:8] * inverse, both[8:16] * inverse
            hid_ref[:, (13 * f + t) * 128 : (13 * f + t + 1) * 128] = (gate / (1.0 + jnp.exp(-gate)) * up).astype(BF16)

    for f in range(2):
        for phase, buffer in (
            (f, a1_recv.at[f, pl.ds(0, 7)]),
            (2 + f, a2_recv.at[f, pl.ds(0, 7)]),
            (7 + f, d1_send.at[f, pl.ds(0, 7)]),
            (9 + f, d1_send.at[f, pl.ds(0, 7)]),
            (11 + f, d3_recv.at[f, pl.ds(0, 7)]),
        ):
            pltpu.make_async_copy(buffer, buffer, send_sem.at[phase]).wait()
    seven = h_recv.at[pl.ds(0, 7)]
    pltpu.make_async_copy(seven, seven, send_sem.at[6]).wait()


def put(so_ref, hid_ref, so_out, hid_out, sem):
    copies = [pltpu.make_async_copy(so_ref, so_out, sem.at[0]), pltpu.make_async_copy(hid_ref, hid_out, sem.at[1])]
    for copy in copies:
        copy.start()
    for copy in copies:
        copy.wait()


def body(stream_in, queries, key_cache, value_cache, lengths, out_weight, norm_gain, gate_weight, up_weight):
    vmem, dma = pltpu.VMEM, pltpu.SemaphoreType.DMA
    residual, hidden = pl.pallas_call(
        kernel,
        out_shape=(vmem((8, 32), BF16), vmem((8, 3328), BF16)),
        in_specs=[pl.BlockSpec(memory_space=pl.ANY)] * 9,
        out_specs=(pl.BlockSpec(memory_space=vmem), pl.BlockSpec(memory_space=vmem)),
        scratch_shapes=[
            vmem((8, 256), BF16),
            vmem((8, 16, 128), BF16),
            vmem((8, 128, 128), BF16),
            vmem((8, 128, 128), BF16),
            pltpu.SMEM((8,), jnp.int32),
            vmem((2048, 256), BF16),
            vmem((256,), BF16),
            vmem((256, 3328), BF16),
            vmem((256, 3328), BF16),
            dma((9,)),
            vmem((2, 80, 128), BF16),
            vmem((2, 8, 80, 128), BF16),
            vmem((2, 80, 128), BF16),
            vmem((2, 8, 80, 128), BF16),
            vmem((128, 128), F32),
            vmem((8, 256), F32),
            vmem((8, 8, 256), F32),
            vmem((2, 8, 16, 256), BF16),
            vmem((2, 8, 16, 256), BF16),
            vmem((2, 16, 256), BF16),
            vmem((2, 8, 16, 256), BF16),
            vmem((2, 16, 256), BF16),
            vmem((2, 8, 16, 256), BF16),
            dma((13,)),
            dma((13,)),
        ],
        compiler_params=pltpu.CompilerParams(
            collective_id=0, has_side_effects=True, vmem_limit_bytes=40 * 1024 * 1024
        ),
        name="decode_step",
    )(
        *(pltpu.with_memory_space_constraint(a, pltpu.HBM) for a in (stream_in, queries[:, 0], key_cache[:, 0], value_cache[:, 0], lengths, out_weight,
        norm_gain, gate_weight, up_weight)),
    )
    return pl.pallas_call(
        put,
        out_shape=(pltpu.HBM((8, 32), BF16), pltpu.HBM((8, 3328), BF16)),
        in_specs=[pl.BlockSpec(memory_space=pl.ANY)] * 2,
        out_specs=(pl.BlockSpec(memory_space=pl.ANY), pl.BlockSpec(memory_space=pl.ANY)),
        scratch_shapes=[dma((2,))],
        name="put",
    )(*(pltpu.with_memory_space_constraint(a, pltpu.VMEM) for a in (residual, hidden)))


def solution(mesh):
    return jax.shard_map(
        body,
        mesh=mesh,
        in_specs=(
            P(None, "kvp"),
            P(None, "head", None, None),
            P(None, "head", "kvp", None),
            P(None, "head", "kvp", None),
            P(),
            P("head", "kvp"),
            P("kvp"),
            P("kvp", "head"),
            P("kvp", "head"),
        ),
        out_specs=(P(None, ("kvp", "head")), P(None, "head")),
        check_vma=False,
    )
```

```python
import jax
import jax.numpy as jnp
from jax import lax
from jax.experimental import pallas as pl
from jax.experimental.pallas import tpu as pltpu
from jax.sharding import PartitionSpec as P

D = 16384
neg_fill = -1e30
epsilon = 1e-05
MESH = pl.DeviceIdType.MESH
F32 = jnp.float32
BF16 = jnp.bfloat16


def merge(parts):
    stats = parts[:, 8].astype(F32)
    shift = jnp.max(stats, axis=0)
    scale = jnp.exp(stats - shift[None])
    weight = jnp.sum(scale * pltpu.roll(stats.reshape(64, 128), 112, 1).reshape(8, 8, 128), axis=0)
    totals = []
    for b in range(8):
        total = None
        for k in range(8):
            term = scale[k, :, stats_lane(b) : stats_lane(b) + 1] * parts[k, b].astype(F32)
            total = term if total is None else total + term
        totals.append(total)
    return totals, shift, weight


def stats_lane(b):
    return 32 * (b // 2) + 8 * (b % 2)


def kernel(
    stream_hbm, q_hbm, k_hbm, v_hbm, len_hbm, ow_hbm, gain_hbm, gw_hbm, uw_hbm,
    so_ref, hid_ref,
    stream_ref, q_ref, k_ref, v_ref, len_ref, ow_ref, gain_ref, gw_ref, uw_ref, in_sem,
    a1_send, a1_recv, a2_send, a2_recv, rows,
    h_send, h_recv, d1_send, d1_recv, d2_send, d2_recv, d3_send, d3_recv,
    send_sem, recv_sem,
):
    kvp, head = lax.axis_index("kvp"), lax.axis_index("head")
    z, y = kvp // 8, lax.rem(kvp, 8)

    def at_z(p):
        return (p * 8 + y, head)

    def at_y(p):
        return (z * 8 + p, head)

    def at_head(p):
        return (kvp, p)

    def place(f):
        return jnp.where(f == 0, z, y)

    def at(f, p):
        return (jnp.where(f == 0, p * 8 + y, z * 8 + p), head)

    def far_first(me, n):
        half = (n + 1) // 2
        return lax.rem(me + jnp.where(lax.rem(n, 2) == 0, 4 + half, 4 - half), 8)

    loads = {}
    for n, (name, src, dst) in enumerate((
        ("k", k_hbm, k_ref), ("q", q_hbm, q_ref), ("len", len_hbm, len_ref), ("v", v_hbm, v_ref),
        ("stream", stream_hbm, stream_ref), ("gain", gain_hbm, gain_ref),
        ("ow", ow_hbm, ow_ref), ("gw", gw_hbm, gw_ref), ("uw", uw_hbm, uw_ref),
    )):
        loads[name] = pltpu.make_async_copy(src, dst, in_sem.at[n])
        if n < 4:
            loads[name].start()

    barrier = pltpu.get_barrier_semaphore()

    @pl.loop(0, 7)
    def _(n):
        for target in (at_z(far_first(z, n)), at_y(far_first(y, n)), at_head(far_first(head, n))):
            pl.semaphore_signal(barrier, inc=1, device_id=target, device_id_type=MESH)

    for name in ("stream", "gain", "ow", "gw", "uw"):
        loads[name].start()

    def send(phase, f, src_of, recv):
        me = place(f)

        @pl.loop(0, 7)
        def _(n):
            p = far_first(me, n)
            pltpu.make_async_remote_copy(
                src_of(p), recv.at[me], send_sem.at[phase], recv_sem.at[phase], device_id=at(f, p), device_id_type=MESH
            ).start()

    def arrived(phase, recv):
        seven = recv.at[pl.ds(0, 7)]
        pltpu.make_async_copy(seven, seven, recv_sem.at[phase]).wait()

    for name in ("len", "q", "k", "v"):
        loads[name].wait()
    position = kvp * 128 + lax.broadcasted_iota(jnp.int32, (16, 128), 1)
    lane = lax.broadcasted_iota(jnp.int32, (8, 128), 1)
    for f in range(2):
        stats = jnp.zeros((8, 128), F32)
        for s in range(4):
            score = lax.dot_general(
                q_ref[4 * f + s], k_ref[4 * f + s], (((1,), (1,)), ((), ())), preferred_element_type=F32
            ) * (128**-0.5)
            inside = position < len_ref[4 * f + s]
            score = jnp.where(inside, score, neg_fill)
            top = jnp.max(score, axis=1, keepdims=True).astype(BF16).astype(F32)
            weight = jnp.where(inside, jnp.exp(score - top), 0.0).astype(BF16)
            weight_sum = jnp.sum(weight.astype(F32), axis=1, keepdims=True)
            total = jnp.dot(weight, v_ref[4 * f + s], preferred_element_type=F32)
            for i in range(2):
                part = slice(8 * i, 8 * i + 8)
                a1_send[f, 2 * s + i] = total[part].astype(BF16)
                stats = jnp.where(lane // 8 == 4 * s + i, top[part], stats)
                stats = jnp.where(lane // 8 == 4 * s + 2 + i, weight_sum[part], stats)
        a1_send[f, 8] = stats.astype(BF16)

    pl.semaphore_wait(barrier, 21)

    @pl.loop(0, 2)
    def _(f):
        send(f, f, lambda p: a1_send.at[f], a1_recv.at[f])
        a1_recv[f, place(f)] = a1_send[f]


    @pl.loop(0, 2)
    def _(f):
        arrived(f, a1_recv.at[f])
        totals, shift, weight = merge(a1_recv[f])
        for b in range(8):
            a2_send[f, b] = totals[b].astype(BF16)
        a2_send[f, 8] = jnp.where(lax.rem(lane // 16, 2) == 0, shift, pltpu.roll(weight, 16, 1)).astype(BF16)
        send(2 + f, 1 - f, lambda p: a2_send.at[f], a2_recv.at[f])
        a2_recv[f, place(1 - f)] = a2_send[f]

    @pl.loop(0, 2)
    def _(f):
        arrived(2 + f, a2_recv.at[f])
        totals, _, weight = merge(a2_recv[f])
        inverse = 1.0 / weight
        for b in range(8):
            rows[pl.ds(64 * f + 8 * b, 8)] = totals[b] * inverse[:, stats_lane(b) : stats_lane(b) + 1]

    loads["ow"].wait()
    loads["stream"].wait()
    loads["gain"].wait()
    attended = jnp.concatenate([rows[pl.ds(j, 8, stride=16), :] for j in range(16)], axis=1).astype(BF16)
    h_send[...] = jnp.dot(attended, ow_ref[...], preferred_element_type=F32)

    @pl.loop(0, 7)
    def _(n):
        p = far_first(head, n)
        pltpu.make_async_remote_copy(
            h_send, h_recv.at[head], send_sem.at[6], recv_sem.at[6], device_id=at_head(p), device_id_type=MESH
        ).start()

    h_recv[head] = h_send[...]
    arrived(6, h_recv)
    projected = jnp.sum(h_recv[...], axis=0)
    stream_out = (stream_ref[...].astype(F32) + projected).astype(BF16)
    widened = stream_out.astype(F32)
    so_ref[...] = pltpu.roll(widened, lax.rem(8 - head, 8) * 32, 1)[:, :32].astype(BF16)
    square = jnp.broadcast_to(jnp.sum(widened * widened, axis=1, keepdims=True), (8, 128))
    scaled = (widened * gain_ref[...].astype(F32).reshape(1, 256)).astype(BF16)

    high = square.astype(BF16)
    squares = jnp.concatenate([square, square - high.astype(F32)], axis=0).astype(BF16)
    for f in range(2):
        d1_send[f, 7] = jnp.concatenate([squares, squares], axis=1)
    loads["gw"].wait()
    loads["uw"].wait()

    def split_squares(f, part):
        square = part[0:8] + part[8:16]
        terms = jnp.concatenate([square, square - square.astype(BF16).astype(F32)], axis=0)
        return jnp.where(place(f) == 7, terms, part).astype(BF16)

    @pl.loop(0, 8)
    def _(n):
        for f in range(2):
            me = place(f)
            p = far_first(me, n)

            @pl.when(p < 7)
            def _():
                columns = pl.ds(pl.multiple_of((13 * f + jnp.minimum(2 * p, 11)) * 128, 128), 256)
                gate = jnp.dot(scaled, gw_ref[:, columns], preferred_element_type=F32)
                up = jnp.dot(scaled, uw_ref[:, columns], preferred_element_type=F32)
                d1_send[f, p] = jnp.concatenate([gate, up], axis=0).astype(BF16)

            @pl.when(n < 7)
            def _():
                pltpu.make_async_remote_copy(
                    d1_send.at[f, p], d1_recv.at[f, me], send_sem.at[7 + f], recv_sem.at[7 + f],
                    device_id=at(f, p), device_id_type=MESH,
                ).start()

    @pl.loop(0, 2)
    def _(f):
        d1_recv[f, place(f)] = d1_send[f, place(f)]
        arrived(7 + f, d1_recv.at[f])
        d2_send[f] = split_squares(f, jnp.sum(d1_recv[f].astype(F32), axis=0))
        send(9 + f, 1 - f, lambda p: d2_send.at[f], d2_recv.at[f])
        d2_recv[f, place(1 - f)] = d2_send[f]

    @pl.loop(0, 2)
    def _(f):
        arrived(9 + f, d2_recv.at[f])
        d3_send[f] = split_squares(f, jnp.sum(d2_recv[f].astype(F32), axis=0))
        send(11 + f, f, lambda p: d3_send.at[f], d3_recv.at[f])
        d3_recv[f, place(f)] = d3_send[f]

    for f in range(2):
        arrived(11 + f, d3_recv.at[f])
    square = d3_recv[0, 7, :, 0:128].astype(F32)
    inverse = lax.rsqrt((square[0:8] + square[8:16]) / D + epsilon)
    for f in range(2):
        for t in range(13):
            k = min(t // 2, 6)
            at_column = (t - min(2 * k, 11)) * 128
            both = d3_recv[f, k, :, at_column : at_column + 128].astype(F32)
            gate, up = both[0:8] * inverse, both[8:16] * inverse
            hid_ref[:, (13 * f + t) * 128 : (13 * f + t + 1) * 128] = (gate / (1.0 + jnp.exp(-gate)) * up).astype(BF16)

    for f in range(2):
        for phase, buffer in (
            (f, a1_recv.at[f, pl.ds(0, 7)]),
            (2 + f, a2_recv.at[f, pl.ds(0, 7)]),
            (7 + f, d1_send.at[f, pl.ds(0, 7)]),
            (9 + f, d1_send.at[f, pl.ds(0, 7)]),
            (11 + f, d3_recv.at[f, pl.ds(0, 7)]),
        ):
            pltpu.make_async_copy(buffer, buffer, send_sem.at[phase]).wait()
    seven = h_recv.at[pl.ds(0, 7)]
    pltpu.make_async_copy(seven, seven, send_sem.at[6]).wait()


def put(so_ref, hid_ref, so_out, hid_out, sem):
    copies = [pltpu.make_async_copy(so_ref, so_out, sem.at[0]), pltpu.make_async_copy(hid_ref, hid_out, sem.at[1])]
    for copy in copies:
        copy.start()
    for copy in copies:
        copy.wait()


def body(stream_in, queries, key_cache, value_cache, lengths, out_weight, norm_gain, gate_weight, up_weight):
    vmem, dma = pltpu.VMEM, pltpu.SemaphoreType.DMA
    residual, hidden = pl.pallas_call(
        kernel,
        out_shape=(vmem((8, 32), BF16), vmem((8, 3328), BF16)),
        in_specs=[pl.BlockSpec(memory_space=pl.ANY)] * 9,
        out_specs=(pl.BlockSpec(memory_space=vmem), pl.BlockSpec(memory_space=vmem)),
        scratch_shapes=[
            vmem((8, 256), BF16),
            vmem((8, 16, 128), BF16),
            vmem((8, 128, 128), BF16),
            vmem((8, 128, 128), BF16),
            pltpu.SMEM((8,), jnp.int32),
            vmem((2048, 256), BF16),
            vmem((256,), BF16),
            vmem((256, 3328), BF16),
            vmem((256, 3328), BF16),
            dma((9,)),
            vmem((2, 9, 8, 128), BF16),
            vmem((2, 8, 9, 8, 128), BF16),
            vmem((2, 9, 8, 128), BF16),
            vmem((2, 8, 9, 8, 128), BF16),
            vmem((128, 128), F32),
            vmem((8, 256), F32),
            vmem((8, 8, 256), F32),
            vmem((2, 8, 16, 256), BF16),
            vmem((2, 8, 16, 256), BF16),
            vmem((2, 16, 256), BF16),
            vmem((2, 8, 16, 256), BF16),
            vmem((2, 16, 256), BF16),
            vmem((2, 8, 16, 256), BF16),
            dma((13,)),
            dma((13,)),
        ],
        compiler_params=pltpu.CompilerParams(
            collective_id=0, has_side_effects=True, vmem_limit_bytes=40 * 1024 * 1024
        ),
        name="decode_step",
    )(
        *(pltpu.with_memory_space_constraint(a, pltpu.HBM) for a in (stream_in, queries[:, 0], key_cache[:, 0], value_cache[:, 0], lengths, out_weight,
        norm_gain, gate_weight, up_weight)),
    )
    return pl.pallas_call(
        put,
        out_shape=(pltpu.HBM((8, 32), BF16), pltpu.HBM((8, 3328), BF16)),
        in_specs=[pl.BlockSpec(memory_space=pl.ANY)] * 2,
        out_specs=(pl.BlockSpec(memory_space=pl.ANY), pl.BlockSpec(memory_space=pl.ANY)),
        scratch_shapes=[dma((2,))],
        name="put",
    )(*(pltpu.with_memory_space_constraint(a, pltpu.VMEM) for a in (residual, hidden)))


def solution(mesh):
    return jax.shard_map(
        body,
        mesh=mesh,
        in_specs=(
            P(None, "kvp"),
            P(None, "head", None, None),
            P(None, "head", "kvp", None),
            P(None, "head", "kvp", None),
            P(),
            P("head", "kvp"),
            P("kvp"),
            P("kvp", "head"),
            P("kvp", "head"),
        ),
        out_specs=(P(None, ("kvp", "head")), P(None, "head")),
        check_vma=False,
    )
```

```python
import jax
import jax.numpy as jnp
from jax import lax
from jax.experimental import pallas as pl
from jax.experimental.pallas import tpu as pltpu
from jax.sharding import PartitionSpec as P

D = 16384
neg_fill = -1e30
epsilon = 1e-05
MESH = pl.DeviceIdType.MESH
F32 = jnp.float32
BF16 = jnp.bfloat16


def merge(parts):
    stats = parts[:, 8].astype(F32)
    shift = jnp.max(stats, axis=0)
    scale = jnp.exp(stats - shift[None])
    weight = jnp.sum(scale * pltpu.roll(stats.reshape(64, 128), 112, 1).reshape(8, 8, 128), axis=0)
    totals = []
    for b in range(8):
        total = None
        for k in range(8):
            term = scale[k, :, stats_lane(b) : stats_lane(b) + 1] * parts[k, b].astype(F32)
            total = term if total is None else total + term
        totals.append(total)
    return totals, shift, weight


def stats_lane(b):
    return 32 * (b // 2) + 8 * (b % 2)


def kernel(
    stream_hbm, q_hbm, k_hbm, v_hbm, len_hbm, ow_hbm, gain_hbm, gw_hbm, uw_hbm,
    so_ref, hid_ref,
    stream_ref, q_ref, k_ref, v_ref, len_ref, ow_ref, gain_ref, gw_ref, uw_ref, in_sem,
    a1_send, a1_recv, a2_send, a2_recv, rows,
    h_send, h_recv, d1_send, d1_recv, d2_send, d2_recv, d3_send, d3_recv,
    send_sem, recv_sem,
):
    kvp, head = lax.axis_index("kvp"), lax.axis_index("head")
    z, y = kvp // 8, lax.rem(kvp, 8)

    def at_z(p):
        return (p * 8 + y, head)

    def at_y(p):
        return (z * 8 + p, head)

    def at_head(p):
        return (kvp, p)

    def place(f):
        return jnp.where(f == 0, z, y)

    def at(f, p):
        return (jnp.where(f == 0, p * 8 + y, z * 8 + p), head)

    def far_first(me, n):
        half = (n + 1) // 2
        return lax.rem(me + jnp.where(lax.rem(n, 2) == 0, 4 + half, 4 - half), 8)

    loads = {}
    for n, (name, src, dst) in enumerate((
        ("k", k_hbm, k_ref), ("q", q_hbm, q_ref), ("len", len_hbm, len_ref), ("v", v_hbm, v_ref),
        ("stream", stream_hbm, stream_ref), ("gain", gain_hbm, gain_ref),
        ("ow", ow_hbm, ow_ref), ("gw", gw_hbm, gw_ref), ("uw", uw_hbm, uw_ref),
    )):
        loads[name] = pltpu.make_async_copy(src, dst, in_sem.at[n])
        if n < 4:
            loads[name].start()

    barrier = pltpu.get_barrier_semaphore()

    @pl.loop(0, 7)
    def _(n):
        for target in (at_z(far_first(z, n)), at_y(far_first(y, n)), at_head(far_first(head, n))):
            pl.semaphore_signal(barrier, inc=1, device_id=target, device_id_type=MESH)

    for name in ("stream", "gain", "ow", "gw", "uw"):
        loads[name].start()

    def send(phase, f, src_of, recv):
        me = place(f)

        @pl.loop(0, 7)
        def _(n):
            p = far_first(me, n)
            pltpu.make_async_remote_copy(
                src_of(p), recv.at[me], send_sem.at[phase], recv_sem.at[phase], device_id=at(f, p), device_id_type=MESH
            ).start()

    def arrived(phase, recv):
        seven = recv.at[pl.ds(0, 7)]
        pltpu.make_async_copy(seven, seven, recv_sem.at[phase]).wait()

    for name in ("len", "q", "k", "v"):
        loads[name].wait()
    position = kvp * 128 + lax.broadcasted_iota(jnp.int32, (16, 128), 1)
    lane = lax.broadcasted_iota(jnp.int32, (8, 128), 1)
    for f in range(2):
        stats = jnp.zeros((8, 128), F32)
        for s in range(4):
            score = lax.dot_general(
                q_ref[4 * f + s], k_ref[4 * f + s], (((1,), (1,)), ((), ())), preferred_element_type=F32
            ) * (128**-0.5)
            inside = position < len_ref[4 * f + s]
            score = jnp.where(inside, score, neg_fill)
            top = jnp.max(score, axis=1, keepdims=True).astype(BF16).astype(F32)
            weight = jnp.where(inside, jnp.exp(score - top), 0.0).astype(BF16)
            weight_sum = jnp.sum(weight.astype(F32), axis=1, keepdims=True)
            total = jnp.dot(weight, v_ref[4 * f + s], preferred_element_type=F32)
            for i in range(2):
                part = slice(8 * i, 8 * i + 8)
                a1_send[f, 2 * s + i] = total[part].astype(BF16)
                stats = jnp.where(lane // 8 == 4 * s + i, top[part], stats)
                stats = jnp.where(lane // 8 == 4 * s + 2 + i, weight_sum[part], stats)
        a1_send[f, 8] = stats.astype(BF16)

    pl.semaphore_wait(barrier, 21)

    @pl.loop(0, 2)
    def _(f):
        send(f, f, lambda p: a1_send.at[f], a1_recv.at[f])
        a1_recv[f, place(f)] = a1_send[f]


    @pl.loop(0, 2)
    def _(f):
        arrived(f, a1_recv.at[f])
        totals, shift, weight = merge(a1_recv[f])
        for b in range(8):
            a2_send[f, b] = totals[b].astype(BF16)
        a2_send[f, 8] = jnp.where(lax.rem(lane // 16, 2) == 0, shift, pltpu.roll(weight, 16, 1)).astype(BF16)
        send(2 + f, 1 - f, lambda p: a2_send.at[f], a2_recv.at[f])
        a2_recv[f, place(1 - f)] = a2_send[f]

    @pl.loop(0, 2)
    def _(f):
        arrived(2 + f, a2_recv.at[f])
        totals, _, weight = merge(a2_recv[f])
        inverse = 1.0 / weight
        for b in range(8):
            rows[pl.ds(64 * f + 8 * b, 8)] = totals[b] * inverse[:, stats_lane(b) : stats_lane(b) + 1]

    loads["ow"].wait()
    loads["stream"].wait()
    loads["gain"].wait()
    attended = jnp.concatenate([rows[pl.ds(j, 8, stride=16), :] for j in range(16)], axis=1).astype(BF16)
    h_send[...] = jnp.dot(attended, ow_ref[...], preferred_element_type=F32)

    @pl.loop(0, 7)
    def _(n):
        p = far_first(head, n)
        pltpu.make_async_remote_copy(
            h_send, h_recv.at[head], send_sem.at[6], recv_sem.at[6], device_id=at_head(p), device_id_type=MESH
        ).start()

    h_recv[head] = h_send[...]
    arrived(6, h_recv)
    projected = jnp.sum(h_recv[...], axis=0)
    stream_out = (stream_ref[...].astype(F32) + projected).astype(BF16)
    widened = stream_out.astype(F32)
    so_ref[...] = pltpu.roll(widened, lax.rem(8 - head, 8) * 32, 1)[:, :32].astype(BF16)
    square = jnp.broadcast_to(jnp.sum(widened * widened, axis=1, keepdims=True), (8, 128))
    scaled = (widened * gain_ref[...].astype(F32).reshape(1, 256)).astype(BF16)

    high = square.astype(BF16)
    squares = jnp.concatenate([square, square - high.astype(F32)], axis=0).astype(BF16)
    for f in range(2):
        d1_send[f, 7] = jnp.concatenate([squares, squares], axis=1)
    loads["gw"].wait()
    loads["uw"].wait()

    def split_squares(f, part):
        square = part[0:8] + part[8:16]
        terms = jnp.concatenate([square, square - square.astype(BF16).astype(F32)], axis=0)
        return jnp.where(place(f) == 7, terms, part).astype(BF16)

    @pl.loop(0, 8)
    def _(n):
        for f in range(2):
            me = place(f)
            p = far_first(me, n)

            @pl.when(p < 7)
            def _():
                columns = pl.ds(pl.multiple_of((13 * f + jnp.minimum(2 * p, 11)) * 128, 128), 256)
                gate = jnp.dot(scaled, gw_ref[:, columns], preferred_element_type=F32)
                up = jnp.dot(scaled, uw_ref[:, columns], preferred_element_type=F32)
                d1_send[f, p] = jnp.concatenate([gate, up], axis=0).astype(BF16)

            @pl.when(n < 7)
            def _():
                pltpu.make_async_remote_copy(
                    d1_send.at[f, p], d1_recv.at[f, me], send_sem.at[7 + f], recv_sem.at[7 + f],
                    device_id=at(f, p), device_id_type=MESH,
                ).start()

    @pl.loop(0, 2)
    def _(f):
        d1_recv[f, place(f)] = d1_send[f, place(f)]
        arrived(7 + f, d1_recv.at[f])
        d2_send[f] = split_squares(f, jnp.sum(d1_recv[f].astype(F32), axis=0))
        send(9 + f, 1 - f, lambda p: d2_send.at[f], d2_recv.at[f])
        d2_recv[f, place(1 - f)] = d2_send[f]

    @pl.loop(0, 2)
    def _(f):
        arrived(9 + f, d2_recv.at[f])
        d3_send[f] = split_squares(f, jnp.sum(d2_recv[f].astype(F32), axis=0))
        me = place(f)

        @pl.loop(0, 7)
        def _(n):
            p = n + jnp.where(n >= me, 1, 0)
            pltpu.make_async_remote_copy(
                d3_send.at[f], d3_recv.at[f, me], send_sem.at[11 + f], recv_sem.at[11 + f],
                device_id=at(f, p), device_id_type=MESH,
            ).start()

        d3_recv[f, place(f)] = d3_send[f]

    for f in range(2):
        for phase, buffer in (
            (f, a1_recv.at[f, pl.ds(0, 7)]),
            (2 + f, a2_recv.at[f, pl.ds(0, 7)]),
            (7 + f, d1_send.at[f, pl.ds(0, 7)]),
            (9 + f, d1_send.at[f, pl.ds(0, 7)]),
            (11 + f, d3_recv.at[f, pl.ds(0, 7)]),
        ):
            pltpu.make_async_copy(buffer, buffer, send_sem.at[phase]).wait()
    seven = h_recv.at[pl.ds(0, 7)]
    pltpu.make_async_copy(seven, seven, send_sem.at[6]).wait()

    for f in range(2):
        arrived(11 + f, d3_recv.at[f])
        if f == 0:
            square = d3_recv[0, 7, :, 0:128].astype(F32)
            inverse = lax.rsqrt((square[0:8] + square[8:16]) / D + epsilon)
        for t in range(13):
            k = min(t // 2, 6)
            at_column = (t - min(2 * k, 11)) * 128
            both = d3_recv[f, k, :, at_column : at_column + 128].astype(F32)
            gate, up = both[0:8] * inverse, both[8:16] * inverse
            hid_ref[:, (13 * f + t) * 128 : (13 * f + t + 1) * 128] = (gate / (1.0 + jnp.exp(-gate)) * up).astype(BF16)


def put(so_ref, hid_ref, so_out, hid_out, sem):
    copies = [pltpu.make_async_copy(so_ref, so_out, sem.at[0]), pltpu.make_async_copy(hid_ref, hid_out, sem.at[1])]
    for copy in copies:
        copy.start()
    for copy in copies:
        copy.wait()


def body(stream_in, queries, key_cache, value_cache, lengths, out_weight, norm_gain, gate_weight, up_weight):
    vmem, dma = pltpu.VMEM, pltpu.SemaphoreType.DMA
    residual, hidden = pl.pallas_call(
        kernel,
        out_shape=(vmem((8, 32), BF16), vmem((8, 3328), BF16)),
        in_specs=[pl.BlockSpec(memory_space=pl.ANY)] * 9,
        out_specs=(pl.BlockSpec(memory_space=vmem), pl.BlockSpec(memory_space=vmem)),
        scratch_shapes=[
            vmem((8, 256), BF16),
            vmem((8, 16, 128), BF16),
            vmem((8, 128, 128), BF16),
            vmem((8, 128, 128), BF16),
            pltpu.SMEM((8,), jnp.int32),
            vmem((2048, 256), BF16),
            vmem((256,), BF16),
            vmem((256, 3328), BF16),
            vmem((256, 3328), BF16),
            dma((9,)),
            vmem((2, 9, 8, 128), BF16),
            vmem((2, 8, 9, 8, 128), BF16),
            vmem((2, 9, 8, 128), BF16),
            vmem((2, 8, 9, 8, 128), BF16),
            vmem((128, 128), F32),
            vmem((8, 256), F32),
            vmem((8, 8, 256), F32),
            vmem((2, 8, 16, 256), BF16),
            vmem((2, 8, 16, 256), BF16),
            vmem((2, 16, 256), BF16),
            vmem((2, 8, 16, 256), BF16),
            vmem((2, 16, 256), BF16),
            vmem((2, 8, 16, 256), BF16),
            dma((13,)),
            dma((13,)),
        ],
        compiler_params=pltpu.CompilerParams(
            collective_id=0, has_side_effects=True, vmem_limit_bytes=40 * 1024 * 1024
        ),
        name="decode_step",
    )(
        *(pltpu.with_memory_space_constraint(a, pltpu.HBM) for a in (stream_in, queries[:, 0], key_cache[:, 0], value_cache[:, 0], lengths, out_weight,
        norm_gain, gate_weight, up_weight)),
    )
    return pl.pallas_call(
        put,
        out_shape=(pltpu.HBM((8, 32), BF16), pltpu.HBM((8, 3328), BF16)),
        in_specs=[pl.BlockSpec(memory_space=pl.ANY)] * 2,
        out_specs=(pl.BlockSpec(memory_space=pl.ANY), pl.BlockSpec(memory_space=pl.ANY)),
        scratch_shapes=[dma((2,))],
        name="put",
    )(*(pltpu.with_memory_space_constraint(a, pltpu.VMEM) for a in (residual, hidden)))


def solution(mesh):
    return jax.shard_map(
        body,
        mesh=mesh,
        in_specs=(
            P(None, "kvp"),
            P(None, "head", None, None),
            P(None, "head", "kvp", None),
            P(None, "head", "kvp", None),
            P(),
            P("head", "kvp"),
            P("kvp"),
            P("kvp", "head"),
            P("kvp", "head"),
        ),
        out_specs=(P(None, ("kvp", "head")), P(None, "head")),
        check_vma=False,
    )
```
